32 devices in a mesh: tile: 16 (over z, y, x), exp: 2 (over core).
Axes of the slice: x: 2, y: 2, z: 4, core: 2. Of those that a mesh axis runs over, the one named last changes fastest.
Arguments:
- initial: float32 [3, 1024, 256], P(None, ('exp', 'tile')), parts along dimension 1, may hold values from -6 to 6
- depth_field: float32 [1024, 256], P(('exp', 'tile')), parts along dimension 0, may hold values from 0.5 to 2
- coriolis: float32 [1024, 256], P(('exp', 'tile')), parts along dimension 0, may hold values from -1 to 1
- cell_area: float32 [1024, 256], P(('exp', 'tile')), parts along dimension 0, may hold values from 1 to 2
- face_len: float32 [2, 1024, 256], P(None, ('exp', 'tile')), parts along dimension 1, may hold values from 0.5 to 1
- owners: int32 [2048, 2], P(('exp', 'tile')), parts along dimension 0, may hold values from 0 to 15, as said below
- offsets: int32 [2048, 2], P(('exp', 'tile')), parts along dimension 0, may hold values from 0 to 15
- weights: bfloat16 [2048, 2, 128, 128], P(('exp', 'tile')), parts along dimension 0, may hold values from -0.25 to 0.25
Outputs:
- remapped: float32 [512, 4, 128], P(('exp', 'tile')), parts along dimension 0
- final_fields: float32 [3, 1024, 256], P(None, ('exp', 'tile')), parts along dimension 1
The draws below stay inside these ranges and needn't reach their ends.
There are 2 independent parts, one for each index of `exp`. The reference program is written for one: setup_inputs(seed, part) draws one part's arguments, and reference() takes and returns one part's arrays. A program takes and returns all parts, laid end to end along the dimension named above; each array names one. Nothing has to cross between parts.
Inputs may be any that keep to these rules, and one draw needn't show every extreme that they name: `owners`: of the 128 intersections of one device's source blocks, at most 16 name the same owner; in every draw one owner is named by exactly 16 intersections of every device.
All inputs are finite; a program needn't handle non-finite values.
Results may differ from the reference program's by a relative error of at most 0.0029.
Values sent between devices are 32-bit elements; how exact they have to be, the bound alone decides.
A program may use at most 64 MiB of HBM per device.

```python
import math
import jax
import jax.numpy as jnp

NY = 256
STEPS = 4
R = 2
TB = 16
SBLK = 64
CAP = 16
NX = 512
SOURCE_BLOCKS = 1024
TBLOCKS = 256
N_TILE = 16


def draw_owners(key, part):
    favored = jax.random.randint(jax.random.fold_in(key, 7), (), 0, N_TILE)
    items_all = jnp.arange(N_TILE * CAP, dtype=jnp.int32)
    owner_of = items_all // CAP
    rank_of = items_all % CAP

    def device_owners(device):
        device_key = jax.random.fold_in(key, device)
        ceiling = jax.random.randint(jax.random.fold_in(device_key, 1), (N_TILE,), CAP // 2, CAP + 1)
        ceiling = jnp.where(jnp.arange(N_TILE) == favored, CAP, ceiling)
        tiebreak = jax.random.permutation(jax.random.fold_in(device_key, 2), N_TILE * CAP)
        grades = jnp.where(owner_of == favored, 0, jnp.where(rank_of < ceiling[owner_of], 1, 2))
        ordering = jnp.argsort(grades * (N_TILE * CAP) + tiebreak)
        picked = ordering[:SBLK * R]
        picked = picked[jax.random.permutation(jax.random.fold_in(device_key, 3), SBLK * R)]
        return (picked // CAP).astype(jnp.int32).reshape(SBLK, R)
    return jax.vmap(device_owners)(jnp.arange(N_TILE)).reshape(N_TILE * SBLK, R)


def plant(array, stream_key, least, largest):
    longest = array.shape.index(max(array.shape))
    spots = []
    for shift in (0, 1):
        where = [jax.random.randint(jax.random.fold_in(stream_key, axis), (), 0, length) for axis, length in enumerate(array.shape)]
        where[longest] = (where[longest] + shift) % array.shape[longest]
        spots.append(tuple(where))
    return array.at[spots[0]].set(least).at[spots[1]].set(largest)


def level_of(stream_key, shape, cuts, smallest, high):
    level = 1.0
    for dim, blocks in cuts:
        steps = jax.random.uniform(jax.random.fold_in(jax.random.fold_in(stream_key, 6), dim), (blocks,), jnp.float32, smallest / len(cuts), high / len(cuts))
        level = level * jnp.repeat(jnp.exp(steps), shape[dim] // blocks).reshape((-1,) + (1,) * (len(shape) - 1 - dim))
    return level


def gaussian(own_key, extent, spread, most, cuts=(), kind=jnp.bfloat16):
    factor_of = level_of(own_key, extent, cuts, -0.22, 0.18) if cuts else 1.0
    result = jax.random.normal(own_key, extent, jnp.float32) * spread * factor_of
    return jnp.minimum(jnp.maximum(result, -most), most).astype(kind)


def setup_inputs(seed: int = 0, part: int = 0) -> dict:
    arg_keys = jax.random.split(jax.random.key(seed), 9)
    own_keys = jax.random.split(jax.random.fold_in(arg_keys[8], part), 9)
    initial = gaussian(own_keys[0], (3, NX, NY), 1.0, 6.0, ((1, 16),), jnp.float32)
    depth_field = jnp.clip(jnp.exp(math.log(2.0) - 1.3862944 * jax.random.uniform(own_keys[1], (NX, NY), jnp.float32) ** level_of(own_keys[1], (NX, NY), ((0, 16),), -0.2, 0.2)), 0.5, 2.0)
    coriolis = jnp.clip(jax.random.uniform(own_keys[2], (NX, NY), jnp.float32, -1.0, 1.0) * level_of(own_keys[2], (NX, NY), ((0, 16),), -0.4, 0.0), -1.0, 1.0)
    cell_area = jnp.clip(1.0 + 1.0 * jax.random.uniform(own_keys[3], (NX, NY), jnp.float32) ** level_of(own_keys[3], (NX, NY), ((0, 16),), -0.2, 0.2), 1.0, 2.0)
    face_len = jnp.clip(0.5 + 0.5 * jax.random.uniform(own_keys[4], (2, NX, NY), jnp.float32) ** level_of(own_keys[4], (2, NX, NY), ((1, 16),), -0.2, 0.2), 0.5, 1.0)
    owners = draw_owners(jax.random.fold_in(jax.random.fold_in(arg_keys[8], part), 71), part)
    offsets = plant(jax.random.randint(own_keys[6], (SOURCE_BLOCKS, R), 0, TB), jax.random.fold_in(own_keys[6], 1), 0, TB - 1).astype(jnp.int32)
    weights = gaussian(own_keys[7], (SOURCE_BLOCKS, R, 128, 128), 512 ** -0.5, 0.25, ((0, 16),))
    return dict(initial=initial, depth_field=depth_field, coriolis=coriolis, cell_area=cell_area, face_len=face_len, owners=owners, offsets=offsets, weights=weights)


time_step = 0.3

def wrapped(values, width):
    return jnp.concatenate([values[:, -width:], values, values[:, :width]], axis=1)

def advance(fields, metric):
    height, speed_x, speed_y = (fields[0], fields[1], fields[2])
    depth, rotation, area, east_len, north_len = (metric[0], metric[1], metric[2], metric[3], metric[4])
    wave_x = jnp.sqrt(jnp.maximum(depth[:-1], depth[1:]))
    edge = east_len[:-1]
    flux_h = edge * (0.5 * (depth[:-1] * speed_x[:-1] + depth[1:] * speed_x[1:]) - 0.5 * wave_x * (height[1:] - height[:-1]))
    flux_u = edge * (0.5 * (height[:-1] + height[1:]) - 0.5 * wave_x * (speed_x[1:] - speed_x[:-1]))
    flux_v = edge * (-0.5 * wave_x * (speed_y[1:] - speed_y[:-1]))
    own_h = height[1:-1]
    own_u = speed_x[1:-1]
    own_v = speed_y[1:-1]
    own_d = depth[1:-1]
    own_f = rotation[1:-1]
    own_a = area[1:-1]
    own_n = north_len[1:-1]
    above_h = jnp.concatenate([own_h[:, 1:], own_h[:, -1:]], axis=1)
    above_u = jnp.concatenate([own_u[:, 1:], own_u[:, -1:]], axis=1)
    above_v = jnp.concatenate([own_v[:, 1:], -own_v[:, -1:]], axis=1)
    above_d = jnp.concatenate([own_d[:, 1:], own_d[:, -1:]], axis=1)
    wave_y = jnp.sqrt(jnp.maximum(own_d, above_d))
    north_h = own_n * (0.5 * (own_d * own_v + above_d * above_v) - 0.5 * wave_y * (above_h - own_h))
    north_u = own_n * (-0.5 * wave_y * (above_u - own_u))
    north_v = own_n * (0.5 * (own_h + above_h) - 0.5 * wave_y * (above_v - own_v))
    wall_v = own_n[:, :1] * (own_h[:, :1] - jnp.sqrt(own_d[:, :1]) * own_v[:, :1])
    zeros = jnp.zeros_like(wall_v)
    south_h = jnp.concatenate([zeros, north_h[:, :-1]], axis=1)
    south_u = jnp.concatenate([zeros, north_u[:, :-1]], axis=1)
    south_v = jnp.concatenate([wall_v, north_v[:, :-1]], axis=1)
    factor = time_step / own_a
    new_h = own_h - factor * (flux_h[1:] - flux_h[:-1] + north_h - south_h)
    new_u = own_u - factor * (flux_u[1:] - flux_u[:-1] + north_u - south_u) + time_step * own_f * own_v
    new_v = own_v - factor * (flux_v[1:] - flux_v[:-1] + north_v - south_v) - time_step * own_f * own_u
    return jnp.stack([new_h, new_u, new_v])

def reference(initial, depth_field, coriolis, cell_area, face_len, owners, offsets, weights):
    metric = jnp.stack([depth_field, coriolis, cell_area, face_len[0], face_len[1]])
    metric_ext = wrapped(metric, 1)
    fields = initial
    snapshots = []
    for number in range(STEPS):
        fields = advance(wrapped(fields, 1), metric_ext)
        snapshots.append(fields[0])
    snapped = jnp.stack(snapshots).astype(jnp.bfloat16)
    blocks = snapped.reshape(STEPS, SOURCE_BLOCKS, 128).astype(jnp.float32)
    contribution = jnp.einsum('sbk,brkt->brst', blocks, weights.astype(jnp.float32))
    target = (owners * TB + offsets).reshape(-1).astype(jnp.int32)
    summed = jax.ops.segment_sum(contribution.reshape(SOURCE_BLOCKS * R, STEPS * 128), target, num_segments=TBLOCKS)
    return (summed.reshape(TBLOCKS, STEPS, 128), fields)
```

```python
import functools

import jax
import jax.numpy as jnp
from jax import lax
from jax.experimental import pallas as pl
from jax.experimental.pallas import tpu as pltpu
from jax.sharding import PartitionSpec as P

STEPS = 4
TB = 16
TIME_STEP = 0.3
INNER = 4
HALO = 4
CHUNKS = ((0, 1), (2, 3))
WEIGHT_PARTS = 4
MESH = pl.DeviceIdType.MESH


def kernel(
    n,
    init_ref,
    depth_ref,
    cor_ref,
    area_ref,
    face_ref,
    own_ref,
    off_ref,
    w_ref,
    out_ref,
    fin_ref,
    st,
    wv,
    hs,
    hr,
    sd,
    cc,
    sel,
    s1,
    r1,
    s2,
    r2,
    load_sem,
    w_sem,
    hs_sem,
    hr_sem,
    s1_sem,
    r1_sem,
    s2_sem,
    r2_sem,
    fin_sem,
):
    cols = init_ref.shape[1]
    ny = init_ref.shape[2]
    ext = cols + 2 * HALO
    blocks = w_ref.shape[0]
    reps = w_ref.shape[1]
    groups = n // INNER
    rows = n * TB
    me = lax.axis_index("tile")
    mine = lax.rem(me, INNER)
    group = me // INNER
    left = lax.rem(me + n - 1, n)
    right = lax.rem(me + 1, n)
    mates = [group * INNER + lax.rem(mine + d, INNER) for d in range(1, INNER)]
    peers = [lax.rem(group + d, groups) * INNER + mine for d in range(1, groups)]

    own_rows = pl.ds(0, cols)
    loads = [
        pltpu.make_async_copy(init_ref, st.at[pl.ds(0, 3), own_rows], load_sem.at[0]),
        pltpu.make_async_copy(depth_ref, st.at[3, own_rows], load_sem.at[1]),
        pltpu.make_async_copy(cor_ref, st.at[4, own_rows], load_sem.at[2]),
        pltpu.make_async_copy(area_ref, st.at[5, own_rows], load_sem.at[3]),
        pltpu.make_async_copy(face_ref, st.at[pl.ds(6, 2), own_rows], load_sem.at[4]),
    ]
    for copy in loads:
        copy.start()
    part = blocks // WEIGHT_PARTS
    w_loads = [
        pltpu.make_async_copy(
            w_ref.at[pl.ds(i * part, part)], wv.at[pl.ds(i * part, part)], w_sem.at[i]
        )
        for i in range(WEIGHT_PARTS)
    ]
    barrier = pltpu.get_barrier_semaphore()
    partners = [left, right] + mates + peers
    for partner in partners:
        pl.semaphore_signal(barrier, inc=1, device_id={"tile": partner}, device_id_type=MESH)
    for copy in w_loads:
        copy.start()
    for copy in loads:
        copy.wait()

    low = lax.broadcasted_iota(jnp.int32, (8, ny), 0) < HALO
    for a in range(4):
        even, odd = st[2 * a, 0:8, :], st[2 * a + 1, 0:8, :]
        hs[0, a] = jnp.where(low, even, pltpu.roll(odd, HALO, 0))
        even, odd = st[2 * a, cols - 8 : cols, :], st[2 * a + 1, cols - 8 : cols, :]
        hs[1, a] = jnp.where(low, pltpu.roll(odd, HALO, 0), even)
    pl.semaphore_wait(barrier, len(partners))
    halos = [
        pltpu.make_async_remote_copy(
            src_ref=hs.at[i],
            dst_ref=hr.at[i],
            send_sem=hs_sem.at[i],
            recv_sem=hr_sem.at[i],
            device_id={"tile": to},
            device_id_type=MESH,
        )
        for i, to in enumerate((left, right))
    ]
    for copy in halos:
        copy.start()

    sd[...] = jnp.zeros_like(sd)
    owner = own_ref[...]
    target = (owner % INNER) * (groups * TB) + (owner // INNER) * TB + off_ref[...]
    place = lax.broadcasted_iota(jnp.int32, (blocks, rows), 1)
    hot = jnp.concatenate(
        [jnp.where(place == target[:, r : r + 1], 1.0, 0.0) for r in range(reps)], axis=0
    )
    hot = hot.T.astype(jnp.bfloat16)
    sel[...] = jnp.concatenate([hot, hot], axis=1)

    for copy in halos:
        copy.wait()
    for a in range(4):
        after, before = hr[0, a], hr[1, a]
        st[2 * a, cols:ext, :] = jnp.where(low, after, before)
        st[2 * a + 1, cols:ext, :] = jnp.where(
            low, pltpu.roll(after, HALO, 0), pltpu.roll(before, HALO, 0)
        )

    def east(x):
        return pltpu.roll(x, ext - 1, 0)

    def west(x):
        return pltpu.roll(x, 1, 0)

    def north(x):
        return pltpu.roll(x, ny - 1, 1)

    def south(x):
        return pltpu.roll(x, 1, 1)

    lane = lax.broadcasted_iota(jnp.int32, (ext, ny), 1)
    first, last = lane == 0, lane == ny - 1
    depth = st[3]
    turn = TIME_STEP * st[4]
    factor = TIME_STEP / st[5]
    half_x = 0.5 * st[6]
    wave_x = half_x * jnp.sqrt(jnp.maximum(depth, east(depth)))
    n_len = st[7]
    half_y = jnp.where(last, 0.0, 0.5 * n_len)
    wave_y = half_y * jnp.sqrt(jnp.maximum(depth, north(depth)))
    wall_h = jnp.where(first, -n_len, jnp.where(last, n_len, 0.0))
    wall_v = jnp.where(first | last, n_len * jnp.sqrt(depth), 0.0)

    def advance(h, u, v):
        q = depth * u
        he, ue, ve = east(h), east(u), east(v)
        fh = half_x * (q + east(q)) - wave_x * (he - h)
        fu = half_x * (h + he) - wave_x * (ue - u)
        fv = wave_x * (v - ve)
        p = depth * v
        hn, un, vn = north(h), north(u), north(v)
        gh = half_y * (p + north(p)) - wave_y * (hn - h)
        gu = wave_y * (u - un)
        gv = half_y * (h + hn) - wave_y * (vn - v)
        new_h = h - factor * (fh - west(fh) + gh - south(gh))
        new_u = u - factor * (fu - west(fu) + gu - south(gu)) + turn * v
        new_v = (
            v - factor * (fv - west(fv) + gv - south(gv) + wall_h * h + wall_v * v) - turn * u
        )
        return new_h, new_u, new_v

    fin_copy = pltpu.make_async_copy(st.at[pl.ds(0, 3), own_rows], fin_ref, fin_sem)

    def remote(src, dst, send, recv, to):
        return pltpu.make_async_remote_copy(
            src_ref=src,
            dst_ref=dst,
            send_sem=send,
            recv_sem=recv,
            device_id={"tile": to},
            device_id_type=MESH,
        )

    inner_copies = [
        [
            remote(
                s1.at[lax.rem(mine + d, INNER), k],
                r1.at[d - 1, k],
                s1_sem.at[d - 1, k],
                r1_sem.at[d - 1, k],
                mates[d - 1],
            )
            for d in range(1, INNER)
        ]
        for k in range(len(CHUNKS))
    ]
    outer_copies = [
        [
            remote(
                s2.at[lax.rem(group + d, groups), k],
                r2.at[d - 1, k],
                s2_sem.at[d - 1, k],
                r2_sem.at[d - 1, k],
                peers[d - 1],
            )
            for d in range(1, groups)
        ]
        for k in range(len(CHUNKS))
    ]

    def second_phase(k):
        for copy in inner_copies[k]:
            copy.wait_recv()
        total = s1[mine, k]
        for d in range(1, INNER):
            total = total + r1[d - 1, k]
        for g in range(groups):
            s2[g, k] = total[:, g * TB : (g + 1) * TB, :]
        for copy in outer_copies[k]:
            copy.start()

    h, u, v = st[0], st[1], st[2]
    for k, chunk in enumerate(CHUNKS):
        for step in chunk:
            h, u, v = advance(h, u, v)
            sd[0, pl.ds(step, cols, stride=8), :] = h[:cols, :128]
            sd[1, pl.ds(STEPS + step, cols, stride=8), :] = h[:cols, 128:]
        if k == len(CHUNKS) - 1:
            st[0], st[1], st[2] = h, u, v
            fin_copy.start()
        if k == 0:
            for copy in w_loads:
                copy.wait()

        def product(c, carry):
            at = pl.ds(pl.multiple_of(c * 8, 8), 8)
            lhs = jnp.concatenate([sd[0, at, :], sd[1, at, :]], axis=1).astype(jnp.bfloat16)
            for r in range(reps):
                rhs = wv[pl.ds(c * 2, 2), r].reshape(256, 128)
                cc[r, at, :] = jnp.dot(lhs, rhs, preferred_element_type=jnp.float32)
            return carry

        lax.fori_loop(0, cols, product, 0, unroll=8)
        high, rest = [], []
        for step in chunk:
            value = jnp.concatenate(
                [cc[r, pl.ds(step, blocks, stride=STEPS), :] for r in range(reps)], axis=0
            )
            top = value.astype(jnp.bfloat16)
            high.append(top)
            rest.append((value - top.astype(jnp.float32)).astype(jnp.bfloat16))
        both = jnp.concatenate(
            [jnp.concatenate(high, axis=1), jnp.concatenate(rest, axis=1)], axis=0
        )
        sums = jnp.dot(sel[...], both, preferred_element_type=jnp.float32)
        for m in range(INNER):
            for i in range(len(chunk)):
                s1[m, k, i] = sums[
                    m * groups * TB : (m + 1) * groups * TB, i * 128 : (i + 1) * 128
                ]
        for copy in inner_copies[k]:
            copy.start()
        if k > 0:
            second_phase(k - 1)
    second_phase(len(CHUNKS) - 1)
    for k, chunk in enumerate(CHUNKS):
        for copy in outer_copies[k]:
            copy.wait_recv()
        total = s2[group, k]
        for d in range(1, groups):
            total = total + r2[d - 1, k]
        for i, step in enumerate(chunk):
            out_ref[:, step, :] = total[i]
    for k in range(len(CHUNKS)):
        for copy in inner_copies[k] + outer_copies[k]:
            copy.wait_send()
    fin_copy.wait()


def on_device(n, initial, depth_field, coriolis, cell_area, face_len, owners, offsets, weights):
    cols, ny = depth_field.shape
    ext = cols + 2 * HALO
    blocks, reps = owners.shape
    groups = n // INNER
    chunks = len(CHUNKS)
    size = len(CHUNKS[0])
    f32 = jnp.float32
    anywhere = pl.BlockSpec(memory_space=pl.ANY)
    vmem = pl.BlockSpec(memory_space=pltpu.VMEM)
    dma = pltpu.SemaphoreType.DMA
    return pl.pallas_call(
        functools.partial(kernel, n),
        out_shape=(
            jax.ShapeDtypeStruct((TB, STEPS, 128), f32),
            jax.ShapeDtypeStruct(initial.shape, f32),
        ),
        in_specs=[anywhere] * 5 + [vmem] * 2 + [anywhere],
        out_specs=(vmem, anywhere),
        scratch_shapes=[
            pltpu.VMEM((8, ext, ny), f32),
            pltpu.VMEM(weights.shape, jnp.bfloat16),
            pltpu.VMEM((2, 4, 8, ny), f32),
            pltpu.VMEM((2, 4, 8, ny), f32),
            pltpu.VMEM((2, cols * 8, 128), f32),
            pltpu.VMEM((reps, cols * 8, 128), f32),
            pltpu.VMEM((n * TB, 2 * blocks * reps), jnp.bfloat16),
            pltpu.VMEM((INNER, chunks, size, groups * TB, 128), f32),
            pltpu.VMEM((INNER - 1, chunks, size, groups * TB, 128), f32),
            pltpu.VMEM((groups, chunks, size, TB, 128), f32),
            pltpu.VMEM((groups - 1, chunks, size, TB, 128), f32),
            dma((5,)),
            dma((WEIGHT_PARTS,)),
            dma((2,)),
            dma((2,)),
            dma((INNER - 1, chunks)),
            dma((INNER - 1, chunks)),
            dma((groups - 1, chunks)),
            dma((groups - 1, chunks)),
            dma,
        ],
        compiler_params=pltpu.CompilerParams(
            collective_id=0, has_side_effects=True, vmem_limit_bytes=40 * 1024 * 1024
        ),
        cost_estimate=pl.CostEstimate(
            flops=2 * weights.size * STEPS, bytes_accessed=2 * weights.size, transcendentals=0
        ),
    )(initial, depth_field, coriolis, cell_area, face_len, owners, offsets, weights)


def solution(mesh):
    columns = ("exp", "tile")
    placed = (
        P(None, columns, None),
        P(columns, None),
        P(columns, None),
        P(columns, None),
        P(None, columns, None),
        P(columns, None),
        P(columns, None),
        P(columns, None, None, None),
    )
    return jax.shard_map(
        functools.partial(on_device, mesh.shape["tile"]),
        mesh=mesh,
        in_specs=placed,
        out_specs=(P(columns, None, None), P(None, columns, None)),
        check_vma=False,
    )
```

```python
import functools

import jax
import jax.numpy as jnp
from jax import lax
from jax.experimental import pallas as pl
from jax.experimental.pallas import tpu as pltpu
from jax.sharding import PartitionSpec as P

STEPS = 4
TB = 16
TIME_STEP = 0.3
INNER = 4
HALO = 4
WEIGHT_PARTS = 4
MESH = pl.DeviceIdType.MESH


def kernel(
    n,
    init_ref,
    depth_ref,
    cor_ref,
    area_ref,
    face_ref,
    own_hbm,
    off_hbm,
    w_ref,
    out_ref,
    fin_ref,
    st,
    own_ref,
    off_ref,
    wv,
    hs,
    hr,
    sd,
    cc,
    sel,
    plane_out,
    plane_in,
    line_out,
    line_in,
    line_out_b,
    line_in_b,
    plane_out_b,
    plane_in_b,
    load_sem,
    w_sem,
    hs_sem,
    hr_sem,
    plane_sems,
    line_sems,
    line_sems_b,
    plane_sems_b,
):
    cols = init_ref.shape[1]
    ny = init_ref.shape[2]
    blocks = w_ref.shape[0]
    reps = w_ref.shape[1]
    groups = n // INNER
    rows = n * TB
    me = lax.axis_index("tile")
    mine = lax.rem(me, INNER)
    group = me // INNER
    left = lax.rem(me + n - 1, n)
    right = lax.rem(me + 1, n)
    mates = [mine + 1 - 2 * lax.rem(mine, 2), lax.rem(mine + 2, INNER), INNER - 1 - mine]
    peers = [lax.rem(group + d, groups) for d in range(1, groups)]
    mate_ids = [group * INNER + m for m in mates]
    peer_ids = [g * INNER + mine for g in peers]

    loads = [
        pltpu.make_async_copy(init_ref, st.at[pl.ds(0, 3)], load_sem.at[0]),
        pltpu.make_async_copy(depth_ref, st.at[3], load_sem.at[1]),
        pltpu.make_async_copy(cor_ref, st.at[4], load_sem.at[2]),
        pltpu.make_async_copy(area_ref, st.at[5], load_sem.at[3]),
        pltpu.make_async_copy(face_ref, st.at[pl.ds(6, 2)], load_sem.at[4]),
    ]
    index_loads = [
        pltpu.make_async_copy(own_hbm, own_ref, load_sem.at[5]),
        pltpu.make_async_copy(off_hbm, off_ref, load_sem.at[6]),
    ]
    for copy in loads + index_loads:
        copy.start()
    part = blocks // WEIGHT_PARTS
    w_loads = [
        pltpu.make_async_copy(
            w_ref.at[pl.ds(i * part, part)], wv.at[pl.ds(i * part, part)], w_sem.at[i]
        )
        for i in range(WEIGHT_PARTS)
    ]
    barrier = pltpu.get_barrier_semaphore()
    partners = [left, right] + mate_ids + peer_ids
    for partner in partners:
        pl.semaphore_signal(barrier, inc=1, device_id={"tile": partner}, device_id_type=MESH)
    for copy in w_loads:
        copy.start()
    for copy in loads:
        copy.wait()

    def remote(src, dst, send, recv, to):
        return pltpu.make_async_remote_copy(
            src_ref=src,
            dst_ref=dst,
            send_sem=send,
            recv_sem=recv,
            device_id={"tile": to},
            device_id_type=MESH,
        )

    low = lax.broadcasted_iota(jnp.int32, (8, ny), 0) < HALO
    for a in range(4):
        even, odd = st[2 * a, 0:8, :], st[2 * a + 1, 0:8, :]
        hs[0, a] = jnp.where(low, even, pltpu.roll(odd, HALO, 0))
        even, odd = st[2 * a, cols - 8 : cols, :], st[2 * a + 1, cols - 8 : cols, :]
        hs[1, a] = jnp.where(low, pltpu.roll(odd, HALO, 0), even)
    pl.semaphore_wait(barrier, len(partners))
    halos = [
        remote(hs.at[i], hr.at[i], hs_sem.at[i], hr_sem.at[i], to)
        for i, to in enumerate((left, right))
    ]
    for copy in halos:
        copy.start()

    def run(fields, keep):
        h, u, v, depth, turn, factor, half_x, n_len = fields
        count = h.shape[0]

        def east(x):
            return pltpu.roll(x, count - 1, 0)

        def west(x):
            return pltpu.roll(x, 1, 0)

        def north(x):
            return pltpu.roll(x, ny - 1, 1)

        def south(x):
            return pltpu.roll(x, 1, 1)

        lane = lax.broadcasted_iota(jnp.int32, (count, ny), 1)
        first, last = lane == 0, lane == ny - 1
        turn = TIME_STEP * turn
        factor = TIME_STEP / factor
        half_x = 0.5 * half_x
        wave_x = half_x * jnp.sqrt(jnp.maximum(depth, east(depth)))
        half_y = jnp.where(last, 0.0, 0.5 * n_len)
        wave_y = half_y * jnp.sqrt(jnp.maximum(depth, north(depth)))
        wall_h = jnp.where(first, -n_len, jnp.where(last, n_len, 0.0))
        wall_v = jnp.where(first | last, n_len * jnp.sqrt(depth), 0.0)
        for step in range(STEPS):
            q = depth * u
            he, ue, ve = east(h), east(u), east(v)
            fh = half_x * (q + east(q)) - wave_x * (he - h)
            fu = half_x * (h + he) - wave_x * (ue - u)
            fv = wave_x * (v - ve)
            p = depth * v
            hn, un, vn = north(h), north(u), north(v)
            gh = half_y * (p + north(p)) - wave_y * (hn - h)
            gu = wave_y * (u - un)
            gv = half_y * (h + hn) - wave_y * (vn - v)
            new_h = h - factor * (fh - west(fh) + gh - south(gh))
            new_u = u - factor * (fu - west(fu) + gu - south(gu)) + turn * v
            new_v = (
                v - factor * (fv - west(fv) + gv - south(gv) + wall_h * h + wall_v * v) - turn * u
            )
            h, u, v = new_h, new_u, new_v
            keep(step, h)
        return h, u, v

    def product(c, carry):
        at = pl.ds(pl.multiple_of(c * 8, 8), 8)
        lhs = jnp.concatenate([sd[0, at, :], sd[1, at, :]], axis=1).astype(jnp.bfloat16)
        for r in range(reps):
            rhs = wv[pl.ds(c * 2, 2), r].reshape(256, 128)
            cc[r, at, :] = jnp.dot(lhs, rhs, preferred_element_type=jnp.float32)
        return carry

    for copy in index_loads:
        copy.wait()
    sd[...] = jnp.zeros_like(sd)
    owner = own_ref[...]
    target = (owner % INNER) * (groups * TB) + (owner // INNER) * TB + off_ref[...]
    place = lax.broadcasted_iota(jnp.int32, (rows, blocks), 0)
    hot = jnp.concatenate(
        [jnp.where(place == target[r : r + 1, :], 1.0, 0.0) for r in range(reps)], axis=1
    ).astype(jnp.bfloat16)
    sel[...] = jnp.concatenate([hot, hot], axis=1)

    def keep_inside(step, h):
        sd[0, pl.ds(step, cols, stride=8), :] = h[:, :128]
        sd[1, pl.ds(STEPS + step, cols, stride=8), :] = h[:, 128:]

    inside = run([st[q] for q in range(8)], keep_inside)
    for q in range(3):
        fin_ref[q] = inside[q]
    for copy in w_loads:
        copy.wait()
    lax.fori_loop(HALO, cols - HALO, product, 0, unroll=8)

    for copy in halos:
        copy.wait()
    edge = []
    for a in range(4):
        after, before = hr[0, a], hr[1, a]
        even = jnp.where(low, after, before)
        odd = jnp.where(low, pltpu.roll(after, HALO, 0), pltpu.roll(before, HALO, 0))
        for q, value in ((2 * a, even), (2 * a + 1, odd)):
            edge.append(
                jnp.concatenate([st[q, cols - 8 : cols, :], value, st[q, 0:8, :]], axis=0)
            )

    def keep_edge(step, h):
        for begin, source in ((0, 16), (cols - HALO, 4)):
            part = h[source : source + HALO]
            sd[0, pl.ds(begin * 8 + step, HALO, stride=8), :] = part[:, :128]
            sd[1, pl.ds(begin * 8 + STEPS + step, HALO, stride=8), :] = part[:, 128:]

    edge = run(edge, keep_edge)
    for c in range(HALO):
        product(c, 0)
        product(cols - HALO + c, 0)

    high, rest = [], []
    for step in range(STEPS):
        value = jnp.concatenate(
            [cc[r, pl.ds(step, blocks, stride=STEPS), :] for r in range(reps)], axis=0
        )
        top = value.astype(jnp.bfloat16)
        high.append(top)
        rest.append((value - top.astype(jnp.float32)).astype(jnp.bfloat16))
    both = jnp.concatenate([jnp.concatenate(high, axis=1), jnp.concatenate(rest, axis=1)], axis=0)
    sums = jnp.dot(sel[...], both, preferred_element_type=jnp.float32)
    for g in range(groups):
        for m in range(INNER):
            at = (m * groups + g) * TB
            line_out_b[g, m] = sums[at : at + TB, :128]
    line_b = [
        remote(line_out_b.at[g], line_in_b.at[d], line_sems_b.at[0, d], line_sems_b.at[1, d], to)
        for d, (g, to) in enumerate(zip(peers, peer_ids))
    ]
    for copy in line_b:
        copy.start()
    for m in range(INNER):
        for i in range(STEPS - 1):
            plane_out[m, i] = sums[
                m * groups * TB : (m + 1) * groups * TB, (i + 1) * 128 : (i + 2) * 128
            ].reshape(groups, TB, 128)
    plane = [
        remote(plane_out.at[m], plane_in.at[d], plane_sems.at[0, d], plane_sems.at[1, d], to)
        for d, (m, to) in enumerate(zip(mates, mate_ids))
    ]
    for copy in reversed(plane):
        copy.start()

    for q in range(3):
        fin_ref[q, 0:HALO, :] = edge[q][16 : 16 + HALO]
        fin_ref[q, cols - HALO : cols, :] = edge[q][4 : 4 + HALO]

    for copy in line_b:
        copy.wait_recv()
    total = line_out_b[group]
    for d in range(groups - 1):
        total = total + line_in_b[d]
    plane_out_b[...] = total
    plane_b = [
        remote(
            plane_out_b.at[m], plane_in_b.at[d], plane_sems_b.at[0, d], plane_sems_b.at[1, d], to
        )
        for d, (m, to) in enumerate(zip(mates, mate_ids))
    ]
    for copy in plane_b:
        copy.start()

    for copy in plane:
        copy.wait_recv()
    for g in range(groups):
        total = plane_out[mine, :, g]
        for d in range(INNER - 1):
            total = total + plane_in[d, :, g]
        line_out[g] = total
    line = [
        remote(line_out.at[g], line_in.at[d], line_sems.at[0, d], line_sems.at[1, d], to)
        for d, (g, to) in enumerate(zip(peers, peer_ids))
    ]
    for copy in line:
        copy.start()

    for copy in plane_b:
        copy.wait_recv()
    total = plane_out_b[mine]
    for d in range(INNER - 1):
        total = total + plane_in_b[d]
    out_ref[:, 0, :] = total
    for copy in line:
        copy.wait_recv()
    total = line_out[group]
    for d in range(groups - 1):
        total = total + line_in[d]
    for i in range(STEPS - 1):
        out_ref[:, i + 1, :] = total[i]
    for copy in plane + line + plane_b + line_b:
        copy.wait_send()


def on_device(n, initial, depth_field, coriolis, cell_area, face_len, owners, offsets, weights):
    cols, ny = depth_field.shape
    blocks, reps = owners.shape
    groups = n // INNER
    f32 = jnp.float32
    hbm = pl.BlockSpec(memory_space=pltpu.HBM)
    vmem = pl.BlockSpec(memory_space=pltpu.VMEM)
    dma = pltpu.SemaphoreType.DMA
    return pl.pallas_call(
        functools.partial(kernel, n),
        out_shape=(
            jax.ShapeDtypeStruct((TB, STEPS, 128), f32),
            jax.ShapeDtypeStruct(initial.shape, f32),
        ),
        in_specs=[hbm] * 8,
        out_specs=(vmem, vmem),
        scratch_shapes=[
            pltpu.VMEM((8, cols, ny), f32),
            pltpu.VMEM((reps, blocks), jnp.int32),
            pltpu.VMEM((reps, blocks), jnp.int32),
            pltpu.VMEM(weights.shape, jnp.bfloat16),
            pltpu.VMEM((2, 4, 8, ny), f32),
            pltpu.VMEM((2, 4, 8, ny), f32),
            pltpu.VMEM((2, cols * 8, 128), f32),
            pltpu.VMEM((reps, cols * 8, 128), f32),
            pltpu.VMEM((n * TB, 2 * blocks * reps), jnp.bfloat16),
            pltpu.VMEM((INNER, STEPS - 1, groups, TB, 128), f32),
            pltpu.VMEM((INNER - 1, STEPS - 1, groups, TB, 128), f32),
            pltpu.VMEM((groups, STEPS - 1, TB, 128), f32),
            pltpu.VMEM((groups - 1, STEPS - 1, TB, 128), f32),
            pltpu.VMEM((groups, INNER, TB, 128), f32),
            pltpu.VMEM((groups - 1, INNER, TB, 128), f32),
            pltpu.VMEM((INNER, TB, 128), f32),
            pltpu.VMEM((INNER - 1, TB, 128), f32),
            dma((7,)),
            dma((WEIGHT_PARTS,)),
            dma((2,)),
            dma((2,)),
            dma((2, INNER - 1)),
            dma((2, groups - 1)),
            dma((2, groups - 1)),
            dma((2, INNER - 1)),
        ],
        compiler_params=pltpu.CompilerParams(
            collective_id=0, has_side_effects=True, vmem_limit_bytes=60 * 1024 * 1024
        ),
        cost_estimate=pl.CostEstimate(
            flops=2 * weights.size * STEPS, bytes_accessed=2 * weights.size, transcendentals=0
        ),
    )(initial, depth_field, coriolis, cell_area, face_len, owners.T, offsets.T, weights)


def solution(mesh):
    columns = ("exp", "tile")
    placed = (
        P(None, columns, None),
        P(columns, None),
        P(columns, None),
        P(columns, None),
        P(None, columns, None),
        P(columns, None),
        P(columns, None),
        P(columns, None, None, None),
    )
    return jax.shard_map(
        functools.partial(on_device, mesh.shape["tile"]),
        mesh=mesh,
        in_specs=placed,
        out_specs=(P(columns, None, None), P(None, columns, None)),
        check_vma=False,
    )
```

```python
import functools

import jax
import jax.numpy as jnp
from jax import lax
from jax.experimental import pallas as pl
from jax.experimental.pallas import tpu as pltpu
from jax.sharding import PartitionSpec as P

STEPS = 4
TB = 16
TIME_STEP = 0.3
INNER = 4
HALO = 4
WEIGHT_PARTS = 4
MESH = pl.DeviceIdType.MESH


def kernel(
    n,
    init_ref,
    depth_ref,
    cor_ref,
    area_ref,
    face_ref,
    own_hbm,
    off_hbm,
    w_ref,
    out_ref,
    fin_ref,
    st,
    own_ref,
    off_ref,
    wv,
    hs,
    hr,
    sd,
    cc,
    sel,
    plane_out,
    plane_in,
    line_out,
    line_in,
    line_out_b,
    line_in_b,
    plane_out_b,
    plane_in_b,
    load_sem,
    w_sem,
    hs_sem,
    hr_sem,
    plane_sems,
    line_sems,
    line_sems_b,
    plane_sems_b,
):
    cols = init_ref.shape[1]
    ny = init_ref.shape[2]
    blocks = w_ref.shape[0]
    reps = w_ref.shape[1]
    groups = n // INNER
    rows = n * TB
    me = lax.axis_index("tile")
    mine = lax.rem(me, INNER)
    group = me // INNER
    left = lax.rem(me + n - 1, n)
    right = lax.rem(me + 1, n)
    mates = [mine + 1 - 2 * lax.rem(mine, 2), lax.rem(mine + 2, INNER), INNER - 1 - mine]
    peers = [lax.rem(group + d, groups) for d in range(1, groups)]
    mate_ids = [group * INNER + m for m in mates]
    peer_ids = [g * INNER + mine for g in peers]

    loads = [
        pltpu.make_async_copy(init_ref, st.at[pl.ds(0, 3)], load_sem.at[0]),
        pltpu.make_async_copy(depth_ref, st.at[3], load_sem.at[1]),
        pltpu.make_async_copy(cor_ref, st.at[4], load_sem.at[2]),
        pltpu.make_async_copy(area_ref, st.at[5], load_sem.at[3]),
        pltpu.make_async_copy(face_ref, st.at[pl.ds(6, 2)], load_sem.at[4]),
    ]
    index_loads = [
        pltpu.make_async_copy(own_hbm, own_ref, load_sem.at[5]),
        pltpu.make_async_copy(off_hbm, off_ref, load_sem.at[6]),
    ]
    for copy in loads + index_loads:
        copy.start()
    part = blocks // WEIGHT_PARTS
    w_loads = [
        pltpu.make_async_copy(
            w_ref.at[pl.ds(i * part, part)], wv.at[pl.ds(i * part, part)], w_sem.at[i]
        )
        for i in range(WEIGHT_PARTS)
    ]
    barrier = pltpu.get_barrier_semaphore()
    partners = [left, right] + mate_ids + peer_ids
    for partner in partners:
        pl.semaphore_signal(barrier, inc=1, device_id={"tile": partner}, device_id_type=MESH)
    for copy in w_loads:
        copy.start()
    for copy in loads:
        copy.wait()

    def remote(src, dst, send, recv, to):
        return pltpu.make_async_remote_copy(
            src_ref=src,
            dst_ref=dst,
            send_sem=send,
            recv_sem=recv,
            device_id={"tile": to},
            device_id_type=MESH,
        )

    low = lax.broadcasted_iota(jnp.int32, (8, ny), 0) < HALO
    for a in range(4):
        even, odd = st[2 * a, 0:8, :], st[2 * a + 1, 0:8, :]
        hs[0, a] = jnp.where(low, even, pltpu.roll(odd, HALO, 0))
        even, odd = st[2 * a, cols - 8 : cols, :], st[2 * a + 1, cols - 8 : cols, :]
        hs[1, a] = jnp.where(low, pltpu.roll(odd, HALO, 0), even)
    pl.semaphore_wait(barrier, len(partners))
    halos = [
        remote(hs.at[i], hr.at[i], hs_sem.at[i], hr_sem.at[i], to)
        for i, to in enumerate((left, right))
    ]
    for copy in halos:
        copy.start()

    def run(fields, keep):
        h, u, v, depth, turn, factor, half_x, n_len = fields
        count = h.shape[0]

        def east(x):
            return pltpu.roll(x, count - 1, 0)

        def west(x):
            return pltpu.roll(x, 1, 0)

        def north(x):
            return pltpu.roll(x, ny - 1, 1)

        def south(x):
            return pltpu.roll(x, 1, 1)

        lane = lax.broadcasted_iota(jnp.int32, (count, ny), 1)
        first, last = lane == 0, lane == ny - 1
        turn = TIME_STEP * turn
        factor = TIME_STEP / factor
        half_x = 0.5 * half_x
        wave_x = half_x * jnp.sqrt(jnp.maximum(depth, east(depth)))
        half_y = jnp.where(last, 0.0, 0.5 * n_len)
        wave_y = half_y * jnp.sqrt(jnp.maximum(depth, north(depth)))
        wall_h = jnp.where(first, -n_len, jnp.where(last, n_len, 0.0))
        wall_v = jnp.where(first | last, n_len * jnp.sqrt(depth), 0.0)
        for step in range(STEPS):
            q = depth * u
            he, ue, ve = east(h), east(u), east(v)
            fh = half_x * (q + east(q)) - wave_x * (he - h)
            fu = half_x * (h + he) - wave_x * (ue - u)
            fv = wave_x * (v - ve)
            p = depth * v
            hn, un, vn = north(h), north(u), north(v)
            gh = half_y * (p + north(p)) - wave_y * (hn - h)
            gu = wave_y * (u - un)
            gv = half_y * (h + hn) - wave_y * (vn - v)
            new_h = h - factor * (fh - west(fh) + gh - south(gh))
            new_u = u - factor * (fu - west(fu) + gu - south(gu)) + turn * v
            new_v = (
                v - factor * (fv - west(fv) + gv - south(gv) + wall_h * h + wall_v * v) - turn * u
            )
            h, u, v = new_h, new_u, new_v
            keep(step, h)
        return h, u, v

    def product(c, carry):
        at = pl.ds(pl.multiple_of(c * 8, 8), 8)
        lhs = jnp.concatenate([sd[0, at, :], sd[1, at, :]], axis=1).astype(jnp.bfloat16)
        for r in range(reps):
            rhs = wv[pl.ds(c * 2, 2), r].reshape(256, 128)
            cc[r, at, :] = jnp.dot(lhs, rhs, preferred_element_type=jnp.float32)
        return carry

    for copy in index_loads:
        copy.wait()
    sd[...] = jnp.zeros_like(sd)
    owner = own_ref[...]
    target = (owner % INNER) * (groups * TB) + (owner // INNER) * TB + off_ref[...]
    place = lax.broadcasted_iota(jnp.int32, (rows, blocks), 0)
    hot = jnp.concatenate(
        [jnp.where(place == target[r : r + 1, :], 1.0, 0.0) for r in range(reps)], axis=1
    ).astype(jnp.bfloat16)
    sel[...] = jnp.concatenate([hot, hot], axis=1)

    def keep_inside(step, h):
        sd[0, pl.ds(step, cols, stride=8), :] = h[:, :128]
        sd[1, pl.ds(STEPS + step, cols, stride=8), :] = h[:, 128:]

    inside = run([st[q] for q in range(8)], keep_inside)
    for q in range(3):
        fin_ref[q] = inside[q]
    for copy in w_loads:
        copy.wait()
    lax.fori_loop(HALO, cols - HALO, product, 0, unroll=8)

    for copy in halos:
        copy.wait()
    edge = []
    for a in range(4):
        after, before = hr[0, a], hr[1, a]
        even = jnp.where(low, after, before)
        odd = jnp.where(low, pltpu.roll(after, HALO, 0), pltpu.roll(before, HALO, 0))
        for q, value in ((2 * a, even), (2 * a + 1, odd)):
            edge.append(
                jnp.concatenate([st[q, cols - 8 : cols, :], value, st[q, 0:8, :]], axis=0)
            )

    def keep_edge(step, h):
        for begin, source in ((0, 16), (cols - HALO, 4)):
            part = h[source : source + HALO]
            sd[0, pl.ds(begin * 8 + step, HALO, stride=8), :] = part[:, :128]
            sd[1, pl.ds(begin * 8 + STEPS + step, HALO, stride=8), :] = part[:, 128:]

    edge = run(edge, keep_edge)
    for c in range(HALO):
        product(c, 0)
        product(cols - HALO + c, 0)

    high, rest = [], []
    for step in range(STEPS):
        value = jnp.concatenate(
            [cc[r, pl.ds(step, blocks, stride=STEPS), :] for r in range(reps)], axis=0
        )
        top = value.astype(jnp.bfloat16)
        high.append(top)
        rest.append((value - top.astype(jnp.float32)).astype(jnp.bfloat16))
    both = jnp.concatenate([jnp.concatenate(high, axis=1), jnp.concatenate(rest, axis=1)], axis=0)
    sums = jnp.dot(sel[...], both, preferred_element_type=jnp.float32)
    for g in range(groups):
        for m in range(INNER):
            at = (m * groups + g) * TB
            line_out_b[g, m] = sums[at : at + TB, :128]
    line_b = [
        remote(line_out_b.at[g], line_in_b.at[d], line_sems_b.at[0, d], line_sems_b.at[1, d], to)
        for d, (g, to) in enumerate(zip(peers, peer_ids))
    ]
    for copy in line_b:
        copy.start()
    for m in range(INNER):
        for i in range(STEPS - 1):
            plane_out[m, i] = sums[
                m * groups * TB : (m + 1) * groups * TB, (i + 1) * 128 : (i + 2) * 128
            ].reshape(groups, TB, 128)
    plane = [
        remote(plane_out.at[m], plane_in.at[d], plane_sems.at[0, d], plane_sems.at[1, d], to)
        for d, (m, to) in enumerate(zip(mates, mate_ids))
    ]
    for copy in reversed(plane):
        copy.start()

    for q in range(3):
        fin_ref[q, 0:HALO, :] = edge[q][16 : 16 + HALO]
        fin_ref[q, cols - HALO : cols, :] = edge[q][4 : 4 + HALO]

    for copy in line_b:
        copy.wait_recv()
    total = line_out_b[group]
    for d in range(groups - 1):
        total = total + line_in_b[d]
    plane_out_b[...] = total
    plane_b = [
        remote(
            plane_out_b.at[m], plane_in_b.at[d], plane_sems_b.at[0, d], plane_sems_b.at[1, d], to
        )
        for d, (m, to) in enumerate(zip(mates, mate_ids))
    ]
    for copy in plane_b:
        copy.start()

    for copy in plane:
        copy.wait_recv()
    for g in range(groups):
        total = plane_out[mine, :, g]
        for d in range(INNER - 1):
            total = total + plane_in[d, :, g]
        line_out[g] = total
    line = [
        remote(line_out.at[g], line_in.at[d], line_sems.at[0, d], line_sems.at[1, d], to)
        for d, (g, to) in enumerate(zip(peers, peer_ids))
    ]
    for copy in line:
        copy.start()

    for copy in plane_b:
        copy.wait_recv()
    total = plane_out_b[mine]
    for d in range(INNER - 1):
        total = total + plane_in_b[d]
    out_ref[:, 0, :] = total
    for copy in line:
        copy.wait_recv()
    total = line_out[group]
    for d in range(groups - 1):
        total = total + line_in[d]
    for i in range(STEPS - 1):
        out_ref[:, i + 1, :] = total[i]
    for copy in plane + line + plane_b + line_b:
        copy.wait_send()


def store(sum_ref, last_ref, out_ref, fin_ref, sems):
    copies = [
        pltpu.make_async_copy(sum_ref, out_ref, sems.at[0]),
        pltpu.make_async_copy(last_ref, fin_ref, sems.at[1]),
    ]
    for copy in copies:
        copy.start()
    for copy in copies:
        copy.wait()


def on_device(n, initial, depth_field, coriolis, cell_area, face_len, owners, offsets, weights):
    cols, ny = depth_field.shape
    blocks, reps = owners.shape
    groups = n // INNER
    f32 = jnp.float32
    hbm = pl.BlockSpec(memory_space=pltpu.HBM)
    vmem = pl.BlockSpec(memory_space=pltpu.VMEM)
    dma = pltpu.SemaphoreType.DMA
    sums, last = pl.pallas_call(
        functools.partial(kernel, n),
        out_shape=(
            pltpu.VMEM((TB, STEPS, 128), f32),
            pltpu.VMEM(initial.shape, f32),
        ),
        in_specs=[hbm] * 8,
        out_specs=(vmem, vmem),
        scratch_shapes=[
            pltpu.VMEM((8, cols, ny), f32),
            pltpu.VMEM((reps, blocks), jnp.int32),
            pltpu.VMEM((reps, blocks), jnp.int32),
            pltpu.VMEM(weights.shape, jnp.bfloat16),
            pltpu.VMEM((2, 4, 8, ny), f32),
            pltpu.VMEM((2, 4, 8, ny), f32),
            pltpu.VMEM((2, cols * 8, 128), f32),
            pltpu.VMEM((reps, cols * 8, 128), f32),
            pltpu.VMEM((n * TB, 2 * blocks * reps), jnp.bfloat16),
            pltpu.VMEM((INNER, STEPS - 1, groups, TB, 128), f32),
            pltpu.VMEM((INNER - 1, STEPS - 1, groups, TB, 128), f32),
            pltpu.VMEM((groups, STEPS - 1, TB, 128), f32),
            pltpu.VMEM((groups - 1, STEPS - 1, TB, 128), f32),
            pltpu.VMEM((groups, INNER, TB, 128), f32),
            pltpu.VMEM((groups - 1, INNER, TB, 128), f32),
            pltpu.VMEM((INNER, TB, 128), f32),
            pltpu.VMEM((INNER - 1, TB, 128), f32),
            dma((7,)),
            dma((WEIGHT_PARTS,)),
            dma((2,)),
            dma((2,)),
            dma((2, INNER - 1)),
            dma((2, groups - 1)),
            dma((2, groups - 1)),
            dma((2, INNER - 1)),
        ],
        compiler_params=pltpu.CompilerParams(
            collective_id=0, has_side_effects=True, vmem_limit_bytes=40 * 1024 * 1024
        ),
        cost_estimate=pl.CostEstimate(
            flops=2 * weights.size * STEPS, bytes_accessed=2 * weights.size, transcendentals=0
        ),
    )(*[pltpu.with_memory_space_constraint(x, pltpu.HBM) for x in (initial, depth_field, coriolis, cell_area, face_len, owners.T, offsets.T, weights)])
    return pl.pallas_call(
        store,
        out_shape=(
            jax.ShapeDtypeStruct(sums.shape, f32),
            jax.ShapeDtypeStruct(last.shape, f32),
        ),
        in_specs=[vmem, vmem],
        out_specs=(hbm, hbm),
        scratch_shapes=[dma((2,))],
    )(
        pltpu.with_memory_space_constraint(sums, pltpu.VMEM),
        pltpu.with_memory_space_constraint(last, pltpu.VMEM),
    )


def solution(mesh):
    columns = ("exp", "tile")
    placed = (
        P(None, columns, None),
        P(columns, None),
        P(columns, None),
        P(columns, None),
        P(None, columns, None),
        P(columns, None),
        P(columns, None),
        P(columns, None, None, None),
    )
    return jax.shard_map(
        functools.partial(on_device, mesh.shape["tile"]),
        mesh=mesh,
        in_specs=placed,
        out_specs=(P(columns, None, None), P(None, columns, None)),
        check_vma=False,
    )
```

```python
import functools

import jax
import jax.numpy as jnp
from jax import lax
from jax.experimental import pallas as pl
from jax.experimental.pallas import tpu as pltpu
from jax.sharding import PartitionSpec as P

STEPS = 4
TB = 16
TIME_STEP = 0.3
INNER = 4
HALO = 4
WEIGHT_PARTS = 4
MESH = pl.DeviceIdType.MESH


def kernel(
    n,
    init_ref,
    depth_ref,
    cor_ref,
    area_ref,
    face_ref,
    own_hbm,
    off_hbm,
    w_ref,
    out_ref,
    fin_ref,
    st,
    own_ref,
    off_ref,
    wv,
    hs,
    hr,
    sd,
    cc,
    sel,
    plane_out,
    plane_in,
    line_out,
    line_in,
    line_out_b,
    line_in_b,
    plane_out_b,
    plane_in_b,
    load_sem,
    w_sem,
    hs_sem,
    hr_sem,
    plane_sems,
    line_sems,
    line_sems_b,
    plane_sems_b,
):
    cols = init_ref.shape[1]
    ny = init_ref.shape[2]
    blocks = w_ref.shape[0]
    reps = w_ref.shape[1]
    groups = n // INNER
    rows = n * TB
    me = lax.axis_index("tile")
    mine = lax.rem(me, INNER)
    group = me // INNER
    left = lax.rem(me + n - 1, n)
    right = lax.rem(me + 1, n)
    mates = [mine + 1 - 2 * lax.rem(mine, 2), lax.rem(mine + 2, INNER), INNER - 1 - mine]
    peers = [lax.rem(group + d, groups) for d in range(1, groups)]
    mate_ids = [group * INNER + m for m in mates]
    peer_ids = [g * INNER + mine for g in peers]

    loads = [
        pltpu.make_async_copy(init_ref, st.at[pl.ds(0, 3)], load_sem.at[0]),
        pltpu.make_async_copy(depth_ref, st.at[3], load_sem.at[1]),
        pltpu.make_async_copy(cor_ref, st.at[4], load_sem.at[2]),
        pltpu.make_async_copy(area_ref, st.at[5], load_sem.at[3]),
        pltpu.make_async_copy(face_ref, st.at[pl.ds(6, 2)], load_sem.at[4]),
    ]
    index_loads = [
        pltpu.make_async_copy(own_hbm, own_ref, load_sem.at[5]),
        pltpu.make_async_copy(off_hbm, off_ref, load_sem.at[6]),
    ]
    for copy in loads + index_loads:
        copy.start()
    part = blocks // WEIGHT_PARTS
    w_loads = [
        pltpu.make_async_copy(
            w_ref.at[pl.ds(i * part, part)], wv.at[pl.ds(i * part, part)], w_sem.at[i]
        )
        for i in range(WEIGHT_PARTS)
    ]
    barrier = pltpu.get_barrier_semaphore()
    partners = [left, right] + mate_ids + peer_ids
    for partner in partners:
        pl.semaphore_signal(barrier, inc=1, device_id={"tile": partner}, device_id_type=MESH)
    for copy in w_loads:
        copy.start()
    for copy in loads:
        copy.wait()

    def remote(src, dst, send, recv, to):
        return pltpu.make_async_remote_copy(
            src_ref=src,
            dst_ref=dst,
            send_sem=send,
            recv_sem=recv,
            device_id={"tile": to},
            device_id_type=MESH,
        )

    low = lax.broadcasted_iota(jnp.int32, (8, ny), 0) < HALO
    for a in range(4):
        even, odd = st[2 * a, 0:8, :], st[2 * a + 1, 0:8, :]
        hs[0, a] = jnp.where(low, even, pltpu.roll(odd, HALO, 0))
        even, odd = st[2 * a, cols - 8 : cols, :], st[2 * a + 1, cols - 8 : cols, :]
        hs[1, a] = jnp.where(low, pltpu.roll(odd, HALO, 0), even)
    pl.semaphore_wait(barrier, len(partners))
    halos = [
        remote(hs.at[i], hr.at[i], hs_sem.at[i], hr_sem.at[i], to)
        for i, to in enumerate((left, right))
    ]
    for copy in halos:
        copy.start()

    def run(fields, keep):
        h, u, v, depth, turn, factor, half_x, n_len = fields
        count = h.shape[0]

        def east(x):
            return pltpu.roll(x, count - 1, 0)

        def west(x):
            return pltpu.roll(x, 1, 0)

        def north(x):
            return pltpu.roll(x, ny - 1, 1)

        def south(x):
            return pltpu.roll(x, 1, 1)

        lane = lax.broadcasted_iota(jnp.int32, (count, ny), 1)
        first, last = lane == 0, lane == ny - 1
        turn = TIME_STEP * turn
        factor = TIME_STEP / factor
        half_x = 0.5 * half_x
        wave_x = half_x * jnp.sqrt(jnp.maximum(depth, east(depth)))
        half_y = jnp.where(last, 0.0, 0.5 * n_len)
        wave_y = half_y * jnp.sqrt(jnp.maximum(depth, north(depth)))
        wall_h = jnp.where(first, -n_len, jnp.where(last, n_len, 0.0))
        wall_v = jnp.where(first | last, n_len * jnp.sqrt(depth), 0.0)
        for step in range(STEPS):
            q = depth * u
            he, ue, ve = east(h), east(u), east(v)
            fh = half_x * (q + east(q)) - wave_x * (he - h)
            fu = half_x * (h + he) - wave_x * (ue - u)
            fv = wave_x * (v - ve)
            p = depth * v
            hn, un, vn = north(h), north(u), north(v)
            gh = half_y * (p + north(p)) - wave_y * (hn - h)
            gu = wave_y * (u - un)
            gv = half_y * (h + hn) - wave_y * (vn - v)
            new_h = h - factor * (fh - west(fh) + gh - south(gh))
            new_u = u - factor * (fu - west(fu) + gu - south(gu)) + turn * v
            new_v = (
                v - factor * (fv - west(fv) + gv - south(gv) + wall_h * h + wall_v * v) - turn * u
            )
            h, u, v = new_h, new_u, new_v
            keep(step, h)
        return h, u, v

    def product(c, carry):
        at = pl.ds(pl.multiple_of(c * 8, 8), 8)
        lhs = jnp.concatenate([sd[0, at, :], sd[1, at, :]], axis=1).astype(jnp.bfloat16)
        for r in range(reps):
            rhs = wv[pl.ds(c * 2, 2), r].reshape(256, 128)
            cc[r, at, :] = jnp.dot(lhs, rhs, preferred_element_type=jnp.float32)
        return carry

    for copy in index_loads:
        copy.wait()
    sd[...] = jnp.zeros_like(sd)
    owner = own_ref[...]
    target = (owner % INNER) * (groups * TB) + (owner // INNER) * TB + off_ref[...]
    place = lax.broadcasted_iota(jnp.int32, (rows, blocks), 0)
    hot = jnp.concatenate(
        [jnp.where(place == target[r : r + 1, :], 1.0, 0.0) for r in range(reps)], axis=1
    ).astype(jnp.bfloat16)
    sel[...] = jnp.concatenate([hot, hot], axis=1)

    def keep_inside(step, h):
        sd[0, pl.ds(step, cols, stride=8), :] = h[:, :128]
        sd[1, pl.ds(STEPS + step, cols, stride=8), :] = h[:, 128:]

    inside = run([st[q] for q in range(8)], keep_inside)
    for q in range(3):
        fin_ref[q] = inside[q]
    for copy in w_loads:
        copy.wait()
    lax.fori_loop(HALO, cols - HALO, product, 0, unroll=8)

    for copy in halos:
        copy.wait()
    edge = []
    for a in range(4):
        after, before = hr[0, a], hr[1, a]
        even = jnp.where(low, after, before)
        odd = jnp.where(low, pltpu.roll(after, HALO, 0), pltpu.roll(before, HALO, 0))
        for q, value in ((2 * a, even), (2 * a + 1, odd)):
            edge.append(
                jnp.concatenate([st[q, cols - 8 : cols, :], value, st[q, 0:8, :]], axis=0)
            )

    def keep_edge(step, h):
        for begin, source in ((0, 16), (cols - HALO, 4)):
            part = h[source : source + HALO]
            sd[0, pl.ds(begin * 8 + step, HALO, stride=8), :] = part[:, :128]
            sd[1, pl.ds(begin * 8 + STEPS + step, HALO, stride=8), :] = part[:, 128:]

    edge = run(edge, keep_edge)
    for c in range(HALO):
        product(c, 0)
        product(cols - HALO + c, 0)

    high, rest = [], []
    for step in range(STEPS):
        value = jnp.concatenate(
            [cc[r, pl.ds(step, blocks, stride=STEPS), :] for r in range(reps)], axis=0
        )
        top = value.astype(jnp.bfloat16)
        high.append(top)
        rest.append((value - top.astype(jnp.float32)).astype(jnp.bfloat16))
    both = jnp.concatenate([jnp.concatenate(high, axis=1), jnp.concatenate(rest, axis=1)], axis=0)
    sums = jnp.dot(sel[...], both[:, :128], preferred_element_type=jnp.float32)
    for g in range(groups):
        for m in range(INNER):
            at = (m * groups + g) * TB
            line_out_b[g, m] = sums[at : at + TB]
    line_b = [
        remote(line_out_b.at[g], line_in_b.at[d], line_sems_b.at[0, d], line_sems_b.at[1, d], to)
        for d, (g, to) in enumerate(zip(peers, peer_ids))
    ]
    for copy in line_b:
        copy.start()
    plane = [
        remote(plane_out.at[m], plane_in.at[d], plane_sems.at[0, d], plane_sems.at[1, d], to)
        for d, (m, to) in enumerate(zip(mates, mate_ids))
    ]
    share = groups * TB
    for m, copy in zip(mates[::-1] + [mine], plane[::-1] + [None]):
        chosen = sel[pl.ds(pl.multiple_of(m * share, share), share), :]
        sums = jnp.dot(chosen, both[:, 128:], preferred_element_type=jnp.float32)
        for i in range(STEPS - 1):
            plane_out[m, i] = sums[:, i * 128 : (i + 1) * 128].reshape(groups, TB, 128)
        if copy is not None:
            copy.start()

    for q in range(3):
        fin_ref[q, 0:HALO, :] = edge[q][16 : 16 + HALO]
        fin_ref[q, cols - HALO : cols, :] = edge[q][4 : 4 + HALO]

    for copy in line_b:
        copy.wait_recv()
    total = line_out_b[group]
    for d in range(groups - 1):
        total = total + line_in_b[d]
    plane_out_b[...] = total
    plane_b = [
        remote(
            plane_out_b.at[m], plane_in_b.at[d], plane_sems_b.at[0, d], plane_sems_b.at[1, d], to
        )
        for d, (m, to) in enumerate(zip(mates, mate_ids))
    ]
    for copy in plane_b:
        copy.start()

    for copy in plane:
        copy.wait_recv()
    line = [
        remote(line_out.at[g], line_in.at[d], line_sems.at[0, d], line_sems.at[1, d], to)
        for d, (g, to) in enumerate(zip(peers, peer_ids))
    ]
    for g, copy in zip(peers + [group], line + [None]):
        total = plane_out[mine, :, g]
        for d in range(INNER - 1):
            total = total + plane_in[d, :, g]
        line_out[g] = total
        if copy is not None:
            copy.start()

    for copy in plane_b:
        copy.wait_recv()
    total = plane_out_b[mine]
    for d in range(INNER - 1):
        total = total + plane_in_b[d]
    out_ref[:, 0, :] = total
    for copy in line:
        copy.wait_recv()
    total = line_out[group]
    for d in range(groups - 1):
        total = total + line_in[d]
    for i in range(STEPS - 1):
        out_ref[:, i + 1, :] = total[i]
    for copy in plane + line + plane_b + line_b:
        copy.wait_send()


def store(sum_ref, last_ref, out_ref, fin_ref, sems):
    copies = [
        pltpu.make_async_copy(sum_ref, out_ref, sems.at[0]),
        pltpu.make_async_copy(last_ref, fin_ref, sems.at[1]),
    ]
    for copy in copies:
        copy.start()
    for copy in copies:
        copy.wait()


def on_device(n, initial, depth_field, coriolis, cell_area, face_len, owners, offsets, weights):
    cols, ny = depth_field.shape
    blocks, reps = owners.shape
    groups = n // INNER
    f32 = jnp.float32
    hbm = pl.BlockSpec(memory_space=pltpu.HBM)
    vmem = pl.BlockSpec(memory_space=pltpu.VMEM)
    dma = pltpu.SemaphoreType.DMA
    sums, last = pl.pallas_call(
        functools.partial(kernel, n),
        out_shape=(
            pltpu.VMEM((TB, STEPS, 128), f32),
            pltpu.VMEM(initial.shape, f32),
        ),
        in_specs=[hbm] * 8,
        out_specs=(vmem, vmem),
        scratch_shapes=[
            pltpu.VMEM((8, cols, ny), f32),
            pltpu.VMEM((reps, blocks), jnp.int32),
            pltpu.VMEM((reps, blocks), jnp.int32),
            pltpu.VMEM(weights.shape, jnp.bfloat16),
            pltpu.VMEM((2, 4, 8, ny), f32),
            pltpu.VMEM((2, 4, 8, ny), f32),
            pltpu.VMEM((2, cols * 8, 128), f32),
            pltpu.VMEM((reps, cols * 8, 128), f32),
            pltpu.VMEM((n * TB, 2 * blocks * reps), jnp.bfloat16),
            pltpu.VMEM((INNER, STEPS - 1, groups, TB, 128), f32),
            pltpu.VMEM((INNER - 1, STEPS - 1, groups, TB, 128), f32),
            pltpu.VMEM((groups, STEPS - 1, TB, 128), f32),
            pltpu.VMEM((groups - 1, STEPS - 1, TB, 128), f32),
            pltpu.VMEM((groups, INNER, TB, 128), f32),
            pltpu.VMEM((groups - 1, INNER, TB, 128), f32),
            pltpu.VMEM((INNER, TB, 128), f32),
            pltpu.VMEM((INNER - 1, TB, 128), f32),
            dma((7,)),
            dma((WEIGHT_PARTS,)),
            dma((2,)),
            dma((2,)),
            dma((2, INNER - 1)),
            dma((2, groups - 1)),
            dma((2, groups - 1)),
            dma((2, INNER - 1)),
        ],
        compiler_params=pltpu.CompilerParams(
            collective_id=0, has_side_effects=True, vmem_limit_bytes=40 * 1024 * 1024
        ),
        cost_estimate=pl.CostEstimate(
            flops=2 * weights.size * STEPS, bytes_accessed=2 * weights.size, transcendentals=0
        ),
    )(*[pltpu.with_memory_space_constraint(x, pltpu.HBM) for x in (initial, depth_field, coriolis, cell_area, face_len, owners.T, offsets.T, weights)])
    return pl.pallas_call(
        store,
        out_shape=(
            jax.ShapeDtypeStruct(sums.shape, f32),
            jax.ShapeDtypeStruct(last.shape, f32),
        ),
        in_specs=[vmem, vmem],
        out_specs=(hbm, hbm),
        scratch_shapes=[dma((2,))],
    )(
        pltpu.with_memory_space_constraint(sums, pltpu.VMEM),
        pltpu.with_memory_space_constraint(last, pltpu.VMEM),
    )


def solution(mesh):
    columns = ("exp", "tile")
    placed = (
        P(None, columns, None),
        P(columns, None),
        P(columns, None),
        P(columns, None),
        P(None, columns, None),
        P(columns, None),
        P(columns, None),
        P(columns, None, None, None),
    )
    return jax.shard_map(
        functools.partial(on_device, mesh.shape["tile"]),
        mesh=mesh,
        in_specs=placed,
        out_specs=(P(columns, None, None), P(None, columns, None)),
        check_vma=False,
    )
```
